32 devices in a mesh: grp: 2 (over x), chol: 16 (over z, y, core).
Axes of the slice: x: 2, y: 2, z: 4, core: 2. Of those that a mesh axis runs over, the one named last changes fastest.
Arguments:
- chol_full: bfloat16 [128, 1024, 1024], P(None, 'chol'), may hold values from -0.015625 to 0.015625
- chol_half: bfloat16 [128, 1024, 256], P(None, 'chol'), may hold values from -0.046875 to 0.046875
- green: bfloat16 [128, 1024, 256], P('grp', 'chol'), parts along dimension 0, may hold values from -6 to 6
- gauss: float32 [128, 128], P('grp'), parts along dimension 0, may hold values from -5 to 5
- orbitals: bfloat16 [128, 1024, 256], P(('grp', 'chol')), parts along dimension 0, may hold values from -6 to 6
Outputs:
- new_orbitals: bfloat16 [128, 1024, 256], P(('grp', 'chol')), parts along dimension 0
- log_factor: float32 [128], P(('grp', 'chol')), parts along dimension 0
The draws below stay inside these ranges and needn't reach their ends.
There are 2 independent parts, one for each index of `grp`. The reference program is written for one: setup_inputs(seed, part) draws one part's arguments, and reference() takes and returns one part's arrays. A program takes and returns all parts, laid end to end along the dimension named above; an argument that names none is the same for every part. Nothing has to cross between parts.
All inputs are finite; a program needn't handle non-finite values.
Results may differ from the reference program's by a relative error of at most 0.0032.
Values may be sent and summed in bfloat16 or wider, within the bound.
No kernel may reach another device: no remote copies, remote signals or barrier semaphores. Data moves between devices by JAX's collectives and lax.ppermute only.
A program may use at most 128 MiB of HBM per device.

```python
import jax
import jax.numpy as jnp
from jax import lax

N = 1024
NOCC = 256
NCH = 128
WALKERS = 64


def raised(drawn, own_key, source, target, parts, factor):
    def block_of(dim):
        return (jnp.arange(drawn.shape[dim]) // (drawn.shape[dim] // parts)).reshape((-1,) + (1,) * (drawn.ndim - 1 - dim))

    one_side = jax.random.permutation(own_key, parts)[block_of(target)]
    other_side = (block_of(target) + parts // 2) % parts
    return jnp.where((block_of(source) == one_side) | (block_of(source) == other_side), factor * drawn, drawn)


def block_scale(rng, dims, shards, smallest, high):
    loudness = 1.0
    for position, blocks in shards:
        steps = jax.random.uniform(jax.random.fold_in(jax.random.fold_in(rng, 6), position), (blocks,), jnp.float32, smallest / len(shards), high / len(shards))
        loudness = loudness * jnp.repeat(jnp.exp(steps), dims[position] // blocks).reshape((-1,) + (1,) * (len(dims) - 1 - position))
    return loudness


def bell_draw(own_key, dims, spread, limit, cuts=(), dtype=jnp.bfloat16):
    entries = spread * jax.random.normal(own_key, dims, jnp.float32)
    if cuts:
        entries = entries * block_scale(own_key, dims, cuts, -0.22, 0.18)
    return jnp.clip(entries, -limit, limit).astype(dtype)


def noise_with(key, dims, deviation, most, shards, heavy, kind=jnp.bfloat16):
    array = deviation * jax.random.normal(key, dims, jnp.float32)
    if shards:
        array = array * block_scale(key, dims, shards, -0.22, 0.18)
    return jnp.clip(raised(array, jax.random.fold_in(key, 3), *heavy), -most, most).astype(kind)


def setup_inputs(seed: int = 0, part: int = 0) -> dict:
    splits = jax.random.split(jax.random.key(seed), 6)
    part_splits = jax.random.split(jax.random.fold_in(splits[5], part), 6)
    return {
        "chol_full": bell_draw(splits[0], (NCH, N, N), (N * NCH) ** -0.5, 0.015625, ((1, 16),)),
        "chol_half": bell_draw(splits[1], (NCH, N, NOCC), (N * NOCC // 16) ** -0.5, 0.046875, ((1, 16),)),
        "green": noise_with(part_splits[2], (WALKERS, N, NOCC), 1.0, 6.0, ((1, 16),), (1, 0, 16, 2.0)),
        "gauss": bell_draw(part_splits[3], (WALKERS, NCH), 1.0, 5.0, (), jnp.float32),
        "orbitals": bell_draw(part_splits[4], (WALKERS, N, NOCC), 1.0, 6.0, ((0, 16),)),
    }


def reference(chol_full, chol_half, green, gauss, orbitals):
    walkers = green.shape[0]
    vbias = jnp.dot(green.reshape(walkers, -1), chol_half.reshape(NCH, -1).T, preferred_element_type=jnp.float32)
    xbar = jnp.clip(-0.3 * vbias, -1.0, 1.0)
    log_factor = jnp.sum(gauss * xbar - 0.5 * xbar * xbar, axis=1)
    fields = (gauss - xbar).astype(jnp.bfloat16)
    flat_chol = chol_full.reshape(NCH, N * N)

    def advance(item):
        field_row, orbit = item
        potential = (jnp.dot(field_row[None, :], flat_chol, preferred_element_type=jnp.float32) * 0.3).astype(jnp.bfloat16)
        potential = potential.reshape(N, N)
        moved = jnp.dot(potential, orbit, preferred_element_type=jnp.float32)
        return (orbit.astype(jnp.float32) + moved).astype(jnp.bfloat16)

    new_orbitals = lax.map(advance, (fields, orbitals))
    return new_orbitals, log_factor
```

```python
import functools

import jax
import jax.numpy as jnp
from jax import lax
from jax.experimental import pallas as pl
from jax.experimental.pallas import tpu as pltpu
from jax.sharding import PartitionSpec as P

PLANES = 4
TILE = 16
VMEM = 40 * 1024 * 1024


def shift_terms(vbias, gauss_rows):
    xbar = jnp.clip(-0.3 * vbias, -1.0, 1.0)
    log_terms = jnp.sum(gauss_rows * xbar - 0.5 * xbar * xbar, axis=1)
    fields = (gauss_rows - xbar).astype(jnp.bfloat16)
    return (fields, log_terms)


def butterfly_sum(value, size):
    step = 1
    while step < size:
        if 2 * step < size:
            one, two, three = (
                lax.ppermute(value, "chol", [(i, i ^ (k * step)) for i in range(size)]) for k in (1, 2, 3)
            )
            value = (value + one) + (two + three)
            step *= 4
        else:
            value = value + lax.ppermute(value, "chol", [(i, i ^ step) for i in range(size)])
            step *= 2
    return value


def potential_kernel(lanes, owned, fields_ref, chol_ref, *rest):
    outs, spread = rest[:lanes], rest[lanes]
    vectors, tile, width = chol_ref.shape

    @pl.when(pl.program_id(0) == 0)
    def _():
        shape = (vectors, vectors * tile)
        pick = lax.broadcasted_iota(jnp.int32, shape, 1) // tile == lax.broadcasted_iota(jnp.int32, shape, 0)
        wide = jnp.dot(fields_ref[...], pick.astype(jnp.bfloat16), preferred_element_type=jnp.float32)
        shape = (tile, vectors * tile)
        mine = lax.broadcasted_iota(jnp.int32, shape, 1) % tile == lax.broadcasted_iota(jnp.int32, shape, 0)
        for w in range(lanes * owned):
            rows = jnp.where(mine, jnp.broadcast_to(wide[w : w + 1], shape), 0.0)
            spread[w * tile : (w + 1) * tile, :] = rows.astype(jnp.bfloat16)

    total = jnp.dot(
        spread[...], chol_ref[...].reshape(vectors * tile, width), preferred_element_type=jnp.float32
    )
    value = (total * 0.3).astype(jnp.bfloat16).reshape(lanes, owned, tile, width)
    for k in range(lanes):
        outs[k][...] = value[k]


def potential_rows(fields, chol_full, lanes):
    vectors, rows, width = chol_full.shape
    walkers = fields.shape[0]
    owned = walkers // lanes
    return pl.pallas_call(
        functools.partial(potential_kernel, lanes, owned),
        grid=(rows // TILE,),
        in_specs=[
            pl.BlockSpec((walkers, vectors), lambda b: (0, 0)),
            pl.BlockSpec((vectors, TILE, width), lambda b: (0, b, 0)),
        ],
        out_specs=[pl.BlockSpec((owned, TILE, width), lambda b: (0, b, 0))] * lanes,
        out_shape=[jax.ShapeDtypeStruct((owned, rows, width), jnp.bfloat16)] * lanes,
        scratch_shapes=[pltpu.VMEM((walkers * TILE, vectors * TILE), jnp.bfloat16)],
        compiler_params=pltpu.CompilerParams(vmem_limit_bytes=VMEM),
        cost_estimate=pl.CostEstimate(
            flops=2 * walkers * TILE * vectors * rows * width,
            bytes_accessed=2 * (vectors + walkers) * rows * width,
            transcendentals=0,
        ),
    )(fields, chol_full)


def moved_kernel(lanes, choices, scalars, *refs):
    pieces, orbs, out = refs[:lanes], refs[lanes : lanes + choices], refs[lanes + choices]
    rows = pieces[0].shape[1]

    def orbital_rows(index):
        if choices == 1:
            return orbs[0][index]
        return jnp.where(scalars[0] == 0, orbs[0][index], orbs[1][index])

    left = jnp.concatenate([piece[0] for piece in pieces], axis=0)
    moved = jnp.dot(left, orbital_rows(0), preferred_element_type=jnp.float32)
    for k in range(lanes):
        lane = lax.rem(scalars[2] + (lanes - k), lanes)
        old = orbital_rows((0, pl.ds(pl.multiple_of((scalars[1] + lane) * rows, rows), rows)))
        new = old.astype(jnp.float32) + moved[k * rows : (k + 1) * rows]
        out[0, pl.ds(pl.multiple_of(lane * rows, rows), rows), :] = new.astype(jnp.bfloat16)


def moved_rows(pieces, orbs, scalars):
    lanes, choices = len(pieces), len(orbs)
    walkers, rows, width = pieces[0].shape
    occupied = orbs[0].shape[2]
    return pl.pallas_call(
        functools.partial(moved_kernel, lanes, choices),
        grid_spec=pltpu.PrefetchScalarGridSpec(
            num_scalar_prefetch=1,
            grid=(walkers,),
            in_specs=[pl.BlockSpec((1, rows, width), lambda w, s: (w, 0, 0))] * lanes
            + [pl.BlockSpec((1, width, occupied), lambda w, s: (w, 0, 0))] * choices,
            out_specs=pl.BlockSpec((1, lanes * rows, occupied), lambda w, s: (w, 0, 0)),
        ),
        out_shape=jax.ShapeDtypeStruct((walkers, lanes * rows, occupied), jnp.bfloat16),
        compiler_params=pltpu.CompilerParams(vmem_limit_bytes=VMEM),
        cost_estimate=pl.CostEstimate(
            flops=2 * walkers * lanes * rows * width * occupied,
            bytes_accessed=2 * walkers * (lanes * rows * (width + occupied) + choices * width * occupied),
            transcendentals=0,
        ),
    )(scalars, *pieces, *orbs)


def join_kernel(scalars, *refs):
    own, beside, sent, cross, mirror, out = refs
    rows = own.shape[1]

    def put(value, k):
        out[0, pl.ds(pl.multiple_of((scalars[1] ^ k) * rows, rows), rows), :] = value

    put(own[0], 0)
    put(jnp.where(scalars[0] == 0, beside[0], sent[0]), 1)
    put(cross[0], 2)
    put(mirror[0], 3)


def join_rows(scalars, blocks):
    walkers, rows, occupied = blocks[0].shape
    return pl.pallas_call(
        join_kernel,
        grid_spec=pltpu.PrefetchScalarGridSpec(
            num_scalar_prefetch=1,
            grid=(walkers,),
            in_specs=[pl.BlockSpec((1, rows, occupied), lambda w, s: (w, 0, 0))] * len(blocks),
            out_specs=pl.BlockSpec((1, PLANES * rows, occupied), lambda w, s: (w, 0, 0)),
        ),
        out_shape=jax.ShapeDtypeStruct((walkers, PLANES * rows, occupied), jnp.bfloat16),
        compiler_params=pltpu.CompilerParams(vmem_limit_bytes=VMEM),
    )(scalars, *blocks)


def on_device(size, chol_full, chol_half, green, gauss, orbitals):
    walkers = green.shape[0]
    owned = orbitals.shape[0]
    vectors = chol_half.shape[0]
    lanes = size // PLANES
    me = lax.axis_index("chol")
    plane, lane = me // lanes, me % lanes
    inner = ((plane == 1) | (plane == 2)).astype(jnp.int32)

    def along(targets):
        return [(a * lanes + k, b * lanes + k) for a, b in targets for k in range(lanes)]

    inward = along([(0, 1), (3, 2)])
    outward = along([(1, 0), (2, 3)])
    middle = along([(1, 2), (2, 1)])

    def send(arrays, targets):
        return [lax.ppermute(a, "chol", targets) for a in arrays]

    parts = 2
    share = owned // parts
    own = [orbitals[i * share : (i + 1) * share] for i in range(parts)]
    beside = send(own, inward)
    facing = send(own, middle)
    far = send(beside, middle)
    out_facing = send(facing, outward)
    out_far = send(far, outward)

    partial_value = lax.dot_general(
        green.reshape(walkers, -1),
        chol_half.reshape(vectors, -1),
        (((1,), (1,)), ((), ())),
        preferred_element_type=jnp.float32,
    )
    vbias = butterfly_sum(partial_value, size)
    fields, log_terms = shift_terms(vbias, gauss)
    log_factor = lax.dynamic_slice_in_dim(log_terms, me * owned, owned, 0)

    fields = fields.reshape(PLANES, lanes * owned, vectors)

    def pieces_of(slot):
        rows = lax.dynamic_index_in_dim(fields, plane ^ slot, 0, keepdims=False)
        rows = jnp.concatenate([rows, rows], axis=0)
        rows = lax.dynamic_slice_in_dim(rows, lane * owned, lanes * owned, 0)
        made = potential_rows(rows, chol_full, lanes)
        return [made[0]] + [
            lax.ppermute(
                made[k], "chol", [(p * lanes + j, p * lanes + (j + k) % lanes) for p in range(PLANES) for j in range(lanes)]
            )
            for k in range(1, lanes)
        ]

    pieces = {slot: pieces_of(slot) for slot in (1, 3, 2, 0)}
    sent = send(pieces[1], inward)

    def scalars(which, rows_of):
        return jnp.stack([which, rows_of * lanes, lane]).astype(jnp.int32)

    def halves(blocks, i):
        return [b[i * share : (i + 1) * share] for b in blocks]

    new = []
    for i in range(parts):
        mirror = moved_rows(halves(pieces[3], i), [out_far[i], facing[i]], scalars(inner, plane))
        cross = moved_rows(halves(pieces[2], i), [out_facing[i], far[i]], scalars(inner, plane))
        next_to = moved_rows(halves(pieces[1], i), [beside[i]], scalars(inner, plane))
        mirror = lax.ppermute(mirror, "chol", along([(0, 3), (3, 0), (1, 2), (2, 1)]))
        cross = lax.ppermute(cross, "chol", along([(0, 2), (2, 0), (1, 3), (3, 1)]))
        next_to = lax.ppermute(next_to, "chol", outward)
        home = moved_rows(halves(pieces[0], i), [own[i]], scalars(inner, plane))
        landed = moved_rows(halves(sent, i), [own[i]], scalars(inner, plane ^ 1))
        new.append(join_rows(jnp.stack([inner, plane]).astype(jnp.int32), [home, next_to, landed, cross, mirror]))
    return (jnp.concatenate(new, axis=0), log_factor)


def solution(mesh):
    placed = (
        P(None, "chol", None),
        P(None, "chol", None),
        P("grp", "chol", None),
        P("grp", None),
        P(("grp", "chol"), None, None),
    )
    return jax.shard_map(
        functools.partial(on_device, mesh.shape["chol"]),
        mesh=mesh,
        in_specs=placed,
        out_specs=(P(("grp", "chol"), None, None), P(("grp", "chol"))),
        check_vma=False,
    )
```

```python
import functools

import jax
import jax.numpy as jnp
from jax import lax
from jax.experimental import pallas as pl
from jax.experimental.pallas import tpu as pltpu
from jax.sharding import PartitionSpec as P

PLANES = 4
TILE = 16
VMEM = 60 * 1024 * 1024


def shift_terms(vbias, gauss_rows):
    xbar = jnp.clip(-0.3 * vbias, -1.0, 1.0)
    log_terms = jnp.sum(gauss_rows * xbar - 0.5 * xbar * xbar, axis=1)
    fields = (gauss_rows - xbar).astype(jnp.bfloat16)
    return (fields, log_terms)


def butterfly_sum(value, size):
    step = 1
    while step < size:
        if 2 * step < size:
            one, two, three = (
                lax.ppermute(value, "chol", [(i, i ^ (k * step)) for i in range(size)]) for k in (1, 2, 3)
            )
            value = (value + one) + (two + three)
            step *= 4
        else:
            value = value + lax.ppermute(value, "chol", [(i, i ^ step) for i in range(size)])
            step *= 2
    return value


def potential_kernel(fields_ref, chol_ref, *rest):
    out, spread = rest[-2:]
    vectors, tile, width = chol_ref.shape
    walkers = fields_ref.shape[0]

    @pl.when(pl.program_id(0) == 0)
    def _():
        shape = (vectors, vectors * tile)
        pick = lax.broadcasted_iota(jnp.int32, shape, 1) // tile == lax.broadcasted_iota(jnp.int32, shape, 0)
        wide = jnp.dot(fields_ref[...], pick.astype(jnp.bfloat16), preferred_element_type=jnp.float32)
        shape = (tile, vectors * tile)
        mine = lax.broadcasted_iota(jnp.int32, shape, 1) % tile == lax.broadcasted_iota(jnp.int32, shape, 0)
        for w in range(walkers):
            rows = jnp.where(mine, jnp.broadcast_to(wide[w : w + 1], shape), 0.0)
            spread[w * tile : (w + 1) * tile, :] = rows.astype(jnp.bfloat16)

    total = jnp.dot(
        spread[...], chol_ref[...].reshape(vectors * tile, width), preferred_element_type=jnp.float32
    )
    out[...] = (total * 0.3).astype(jnp.bfloat16).reshape(walkers, tile, width)


def potential_rows(fields, chol_full, after):
    vectors, rows, width = chol_full.shape
    walkers = fields.shape[0]
    return pl.pallas_call(
        potential_kernel,
        grid=(rows // TILE,),
        in_specs=[
            pl.BlockSpec((walkers, vectors), lambda b: (0, 0)),
            pl.BlockSpec((vectors, TILE, width), lambda b: (0, b, 0)),
        ]
        + [pl.BlockSpec(memory_space=pl.ANY)] * len(after),
        out_specs=pl.BlockSpec((walkers, TILE, width), lambda b: (0, b, 0)),
        out_shape=jax.ShapeDtypeStruct((walkers, rows, width), jnp.bfloat16),
        scratch_shapes=[pltpu.VMEM((walkers * TILE, vectors * TILE), jnp.bfloat16)],
        compiler_params=pltpu.CompilerParams(vmem_limit_bytes=VMEM),
        cost_estimate=pl.CostEstimate(flops=60_000_000_000, bytes_accessed=1, transcendentals=0),
    )(fields, chol_full, *after)


def copy_kernel(source, *rest):
    rest[-1][...] = source[...]


def some_walkers(orbitals, first, walkers, after):
    _, width, occupied = orbitals.shape
    return pl.pallas_call(
        copy_kernel,
        grid=(walkers,),
        in_specs=[pl.BlockSpec((1, width, occupied), lambda w: (w + first, 0, 0))]
        + [pl.BlockSpec(memory_space=pl.ANY)] * len(after),
        out_specs=pl.BlockSpec((1, width, occupied), lambda w: (w, 0, 0)),
        out_shape=jax.ShapeDtypeStruct((walkers, width, occupied), orbitals.dtype),
        compiler_params=pltpu.CompilerParams(vmem_limit_bytes=VMEM),
        cost_estimate=pl.CostEstimate(flops=1, bytes_accessed=1, transcendentals=0),
    )(orbitals, *after)


def moved_kernel(choices, scalars, pieces, *refs):
    orbs, out = refs[:choices], refs[-1]
    rows = out.shape[1]

    def orbital_rows(index):
        if choices == 1:
            return orbs[0][index]
        return jnp.where(scalars[0] == 0, orbs[0][index], orbs[1][index])

    left = pieces[...].reshape(rows, pieces.shape[3])
    moved = jnp.dot(left, orbital_rows(0), preferred_element_type=jnp.float32)
    old = orbital_rows((0, pl.ds(pl.multiple_of(scalars[1] * rows, rows), rows)))
    out[0] = (old.astype(jnp.float32) + moved).astype(jnp.bfloat16)


def moved_rows(pieces, orbs, scalars, first, after=()):
    choices = len(orbs)
    lanes, _, rows, width = pieces.shape
    walkers, _, occupied = orbs[0].shape
    return pl.pallas_call(
        functools.partial(moved_kernel, choices),
        grid_spec=pltpu.PrefetchScalarGridSpec(
            num_scalar_prefetch=1,
            grid=(walkers,),
            in_specs=[pl.BlockSpec((lanes, 1, rows, width), lambda w, s: (0, w + first, 0, 0))]
            + [pl.BlockSpec((1, width, occupied), lambda w, s: (w, 0, 0))] * choices
            + [pl.BlockSpec(memory_space=pl.ANY)] * len(after),
            out_specs=pl.BlockSpec((1, lanes * rows, occupied), lambda w, s: (w, 0, 0)),
        ),
        out_shape=jax.ShapeDtypeStruct((walkers, lanes * rows, occupied), jnp.bfloat16),
        compiler_params=pltpu.CompilerParams(vmem_limit_bytes=VMEM),
        cost_estimate=pl.CostEstimate(flops=15_000_000_000, bytes_accessed=1, transcendentals=0),
    )(scalars, pieces, *orbs, *after)


def join_kernel(scalars, *refs):
    own, beside, sent, cross, mirror, out = refs
    rows = own.shape[1]

    def put(value, k):
        out[0, pl.ds(pl.multiple_of((scalars[1] ^ k) * rows, rows), rows), :] = value

    put(own[0], 0)
    put(jnp.where(scalars[0] == 0, beside[0], sent[0]), 1)
    put(cross[0], 2)
    put(mirror[0], 3)


def join_rows(scalars, blocks):
    walkers, rows, occupied = blocks[0].shape
    return pl.pallas_call(
        join_kernel,
        grid_spec=pltpu.PrefetchScalarGridSpec(
            num_scalar_prefetch=1,
            grid=(walkers,),
            in_specs=[pl.BlockSpec((1, rows, occupied), lambda w, s: (w, 0, 0))] * len(blocks),
            out_specs=pl.BlockSpec((1, PLANES * rows, occupied), lambda w, s: (w, 0, 0)),
        ),
        out_shape=jax.ShapeDtypeStruct((walkers, PLANES * rows, occupied), jnp.bfloat16),
        compiler_params=pltpu.CompilerParams(vmem_limit_bytes=VMEM),
    )(scalars, *blocks)


def on_device(size, chol_full, chol_half, green, gauss, orbitals):
    walkers = green.shape[0]
    owned = orbitals.shape[0]
    vectors = chol_half.shape[0]
    lanes = size // PLANES
    me = lax.axis_index("chol")
    plane, lane = me // lanes, me % lanes
    inner = ((plane == 1) | (plane == 2)).astype(jnp.int32)

    def along(targets):
        return [(a * lanes + k, b * lanes + k) for a, b in targets for k in range(lanes)]

    inward = along([(0, 1), (3, 2)])
    outward = along([(1, 0), (2, 3)])
    middle = along([(1, 2), (2, 1)])

    def send(arrays, targets):
        return [lax.ppermute(a, "chol", targets) for a in arrays]

    parts = 2
    share = owned // parts

    def forward(mine):
        beside, facing = send([mine], inward), send([mine], middle)
        far, out_facing = send(beside, middle), send(facing, outward)
        return mine, beside[0], facing[0], far[0], out_facing[0], send(far, outward)[0]

    halves = [forward(some_walkers(orbitals, 0, share, []))]

    partial_value = lax.dot_general(
        green.reshape(walkers, -1),
        chol_half.reshape(vectors, -1),
        (((1,), (1,)), ((), ())),
        preferred_element_type=jnp.float32,
    )
    vbias = butterfly_sum(partial_value, size)
    fields, log_terms = shift_terms(vbias, gauss)
    log_factor = lax.dynamic_slice_in_dim(log_terms, me * owned, owned, 0)
    fields = fields.reshape(PLANES, lanes * owned, vectors)
    rows, width = chol_full.shape[1:]
    groups = [[p * lanes + k for k in range(lanes)] for p in range(PLANES)]

    def made_for(slot, after):
        return potential_rows(lax.dynamic_index_in_dim(fields, plane ^ slot, 0, keepdims=False), chol_full, after)

    def exchange(made):
        return lax.all_to_all(made, "chol", 0, 0, axis_index_groups=groups, tiled=True).reshape(lanes, owned, rows, width)

    def scalars(rows_of):
        return jnp.stack([inner, rows_of]).astype(jnp.int32)

    def moved(pieces, choices, rows_of, i, after=()):
        return moved_rows(pieces, choices, scalars(rows_of), i * share, after)

    first, second = range(parts)
    made = made_for(1, [halves[0][1], halves[0][2]])
    halves.append(forward(some_walkers(orbitals, share, share, [made])))
    own, beside, facing, far, out_facing, out_far = zip(*halves)
    pieces = exchange(made)
    (sent,) = send([pieces], inward)
    next_to = [moved(pieces, [beside[i]], plane, i) for i in range(parts)]
    pieces = exchange(made_for(3, [far[first], out_facing[first]]))
    mirror = [moved(pieces, [out_far[i], facing[i]], plane, i) for i in range(parts)]
    pieces = exchange(made_for(2, [facing[second], beside[second], out_far[first]]))
    cross = [moved(pieces, [out_facing[i], far[i]], plane, i, [out_far[second]]) for i in range(parts)]
    pieces = exchange(made_for(0, [far[second], out_facing[second], *next_to, mirror[first]]))
    mirror = send(mirror, along([(0, 3), (3, 0), (1, 2), (2, 1)]))
    cross = send(cross, along([(0, 2), (2, 0), (1, 3), (3, 1)]))
    next_to = send(next_to, outward)
    new = []
    for i in range(parts):
        home = moved(pieces, [own[i]], plane, i)
        landed = moved(sent, [own[i]], plane ^ 1, i)
        new.append(join_rows(scalars(plane), [home, next_to[i], landed, cross[i], mirror[i]]))
    return (jnp.concatenate(new, axis=0), log_factor)


def solution(mesh):
    placed = (
        P(None, "chol", None),
        P(None, "chol", None),
        P("grp", "chol", None),
        P("grp", None),
        P(("grp", "chol"), None, None),
    )
    return jax.shard_map(
        functools.partial(on_device, mesh.shape["chol"]),
        mesh=mesh,
        in_specs=placed,
        out_specs=(P(("grp", "chol"), None, None), P(("grp", "chol"))),
        check_vma=False,
    )
```

```python
import functools

import jax
import jax.numpy as jnp
from jax import lax
from jax.experimental import pallas as pl
from jax.experimental.pallas import tpu as pltpu
from jax.sharding import PartitionSpec as P

PLANES = 4
TILE = 16
VMEM = 60 * 1024 * 1024


def shift_terms(vbias, gauss_rows):
    xbar = jnp.clip(-0.3 * vbias, -1.0, 1.0)
    log_terms = jnp.sum(gauss_rows * xbar - 0.5 * xbar * xbar, axis=1)
    fields = (gauss_rows - xbar).astype(jnp.bfloat16)
    return (fields, log_terms)


def butterfly_sum(value, size):
    step = 1
    while step < size:
        if 2 * step < size:
            one, two, three = (
                lax.ppermute(value, "chol", [(i, i ^ (k * step)) for i in range(size)]) for k in (1, 2, 3)
            )
            value = (value + one) + (two + three)
            step *= 4
        else:
            value = value + lax.ppermute(value, "chol", [(i, i ^ step) for i in range(size)])
            step *= 2
    return value


def potential_kernel(slots, fields_ref, chol_ref, *rest):
    outs, spread = rest[-1 - slots : -1], rest[-1]
    vectors, tile, width = chol_ref.shape
    walkers = fields_ref.shape[0]

    @pl.when(pl.program_id(0) == 0)
    def _():
        shape = (vectors, vectors * tile)
        pick = lax.broadcasted_iota(jnp.int32, shape, 1) // tile == lax.broadcasted_iota(jnp.int32, shape, 0)
        wide = jnp.dot(fields_ref[...], pick.astype(jnp.bfloat16), preferred_element_type=jnp.float32)
        shape = (tile, vectors * tile)
        mine = lax.broadcasted_iota(jnp.int32, shape, 1) % tile == lax.broadcasted_iota(jnp.int32, shape, 0)
        for w in range(walkers):
            rows = jnp.where(mine, jnp.broadcast_to(wide[w : w + 1], shape), 0.0)
            spread[w * tile : (w + 1) * tile, :] = rows.astype(jnp.bfloat16)

    total = jnp.dot(
        spread[...], chol_ref[...].reshape(vectors * tile, width), preferred_element_type=jnp.float32
    )
    value = (total * 0.3).astype(jnp.bfloat16).reshape(slots, walkers // slots, tile, width)
    for i in range(slots):
        outs[i][...] = value[i]


def potential_rows(fields, chol_full, after):
    vectors, rows, width = chol_full.shape
    slots, share = len(fields), fields[0].shape[0]
    walkers = slots * share
    return pl.pallas_call(
        functools.partial(potential_kernel, slots),
        grid=(rows // TILE,),
        in_specs=[
            pl.BlockSpec((walkers, vectors), lambda b: (0, 0)),
            pl.BlockSpec((vectors, TILE, width), lambda b: (0, b, 0)),
        ]
        + [pl.BlockSpec(memory_space=pl.ANY)] * len(after),
        out_specs=[pl.BlockSpec((share, TILE, width), lambda b: (0, b, 0))] * slots,
        out_shape=[jax.ShapeDtypeStruct((share, rows, width), jnp.bfloat16)] * slots,
        scratch_shapes=[pltpu.VMEM((walkers * TILE, vectors * TILE), jnp.bfloat16)],
        compiler_params=pltpu.CompilerParams(vmem_limit_bytes=VMEM),
        cost_estimate=pl.CostEstimate(flops=60_000_000_000, bytes_accessed=1, transcendentals=0),
    )(jnp.concatenate(fields, axis=0), chol_full, *after)


def copy_kernel(source, *rest):
    rest[-1][...] = source[...]


def some_walkers(orbitals, first, walkers, after):
    _, width, occupied = orbitals.shape
    return pl.pallas_call(
        copy_kernel,
        grid=(walkers,),
        in_specs=[pl.BlockSpec((1, width, occupied), lambda w: (w + first, 0, 0))]
        + [pl.BlockSpec(memory_space=pl.ANY)] * len(after),
        out_specs=pl.BlockSpec((1, width, occupied), lambda w: (w, 0, 0)),
        out_shape=jax.ShapeDtypeStruct((walkers, width, occupied), orbitals.dtype),
        compiler_params=pltpu.CompilerParams(vmem_limit_bytes=VMEM),
        cost_estimate=pl.CostEstimate(flops=1, bytes_accessed=1, transcendentals=0),
    )(orbitals, *after)


def moved_kernel(choices, scalars, pieces, *refs):
    orbs, out = refs[:choices], refs[-1]
    rows = out.shape[1]

    def orbital_rows(index):
        if choices == 1:
            return orbs[0][index]
        return jnp.where(scalars[0] == 0, orbs[0][index], orbs[1][index])

    left = pieces[...].reshape(rows, pieces.shape[3])
    moved = jnp.dot(left, orbital_rows(0), preferred_element_type=jnp.float32)
    old = orbital_rows((0, pl.ds(pl.multiple_of(scalars[1] * rows, rows), rows)))
    out[0] = (old.astype(jnp.float32) + moved).astype(jnp.bfloat16)


def moved_rows(pieces, orbs, scalars, first, after=()):
    choices = len(orbs)
    lanes, _, rows, width = pieces.shape
    walkers, _, occupied = orbs[0].shape
    return pl.pallas_call(
        functools.partial(moved_kernel, choices),
        grid_spec=pltpu.PrefetchScalarGridSpec(
            num_scalar_prefetch=1,
            grid=(walkers,),
            in_specs=[pl.BlockSpec((lanes, 1, rows, width), lambda w, s: (0, w + first, 0, 0))]
            + [pl.BlockSpec((1, width, occupied), lambda w, s: (w, 0, 0))] * choices
            + [pl.BlockSpec(memory_space=pl.ANY)] * len(after),
            out_specs=pl.BlockSpec((1, lanes * rows, occupied), lambda w, s: (w, 0, 0)),
        ),
        out_shape=jax.ShapeDtypeStruct((walkers, lanes * rows, occupied), jnp.bfloat16),
        compiler_params=pltpu.CompilerParams(vmem_limit_bytes=VMEM),
        cost_estimate=pl.CostEstimate(flops=15_000_000_000, bytes_accessed=1, transcendentals=0),
    )(scalars, pieces, *orbs, *after)


def join_kernel(parts, scalars, *refs):
    out = refs[-1]
    rows = refs[0].shape[1]
    share = refs[0].shape[0]

    for part in range(parts):
        own, beside, sent, cross, mirror = refs[part * 5 : part * 5 + 5]
        walkers = pl.ds(part * share, share)

        def put(value, k):
            out[walkers, pl.ds(pl.multiple_of((scalars[1] ^ k) * rows, rows), rows), :] = value

        put(own[...], 0)
        put(jnp.where(scalars[0] == 0, beside[...], sent[...]), 1)
        put(cross[...], 2)
        put(mirror[...], 3)


def join_rows(scalars, parts):
    walkers, rows, occupied = parts[0][0].shape
    columns = 128 if occupied % 128 == 0 else occupied
    return pl.pallas_call(
        functools.partial(join_kernel, len(parts)),
        grid_spec=pltpu.PrefetchScalarGridSpec(
            num_scalar_prefetch=1,
            grid=(occupied // columns,),
            in_specs=[pl.BlockSpec((walkers, rows, columns), lambda c, s: (0, 0, c))] * (5 * len(parts)),
            out_specs=pl.BlockSpec((len(parts) * walkers, PLANES * rows, columns), lambda c, s: (0, 0, c)),
        ),
        out_shape=jax.ShapeDtypeStruct((len(parts) * walkers, PLANES * rows, occupied), jnp.bfloat16),
        compiler_params=pltpu.CompilerParams(vmem_limit_bytes=VMEM),
    )(scalars, *(block for part in parts for block in part))


def on_device(size, chol_full, chol_half, green, gauss, orbitals):
    walkers = green.shape[0]
    owned = orbitals.shape[0]
    vectors = chol_half.shape[0]
    lanes = size // PLANES
    me = lax.axis_index("chol")
    plane, lane = me // lanes, me % lanes
    inner = ((plane == 1) | (plane == 2)).astype(jnp.int32)

    def along(targets):
        return [(a * lanes + k, b * lanes + k) for a, b in targets for k in range(lanes)]

    inward = along([(0, 1), (3, 2)])
    outward = along([(1, 0), (2, 3)])
    middle = along([(1, 2), (2, 1)])

    def send(arrays, targets):
        return [lax.ppermute(a, "chol", targets) for a in arrays]

    parts = 2
    share = owned // parts

    def forward(mine):
        beside, facing = send([mine], inward), send([mine], middle)
        far, out_facing = send(beside, middle), send(facing, outward)
        return mine, beside[0], facing[0], far[0], out_facing[0], send(far, outward)[0]

    halves = [forward(some_walkers(orbitals, 0, share, []))]

    partial_value = lax.dot_general(
        green.reshape(walkers, -1),
        chol_half.reshape(vectors, -1),
        (((1,), (1,)), ((), ())),
        preferred_element_type=jnp.float32,
    )
    vbias = butterfly_sum(partial_value, size)
    fields, log_terms = shift_terms(vbias, gauss)
    log_factor = lax.dynamic_slice_in_dim(log_terms, me * owned, owned, 0)
    fields = fields.reshape(PLANES, lanes * owned, vectors)
    rows, width = chol_full.shape[1:]
    groups = [[p * lanes + k for k in range(lanes)] for p in range(PLANES)]

    def made_for(slots, after):
        chosen = [lax.dynamic_index_in_dim(fields, plane ^ slot, 0, keepdims=False) for slot in slots]
        return potential_rows(chosen, chol_full, after)

    def exchange(made):
        return lax.all_to_all(made, "chol", 0, 0, axis_index_groups=groups, tiled=True).reshape(lanes, owned, rows, width)

    def scalars(rows_of):
        return jnp.stack([inner, rows_of]).astype(jnp.int32)

    def moved(pieces, choices, rows_of, i, after=()):
        return moved_rows(pieces, choices, scalars(rows_of), i * share, after)

    first, second = range(parts)
    (made,) = made_for((1,), [halves[0][1], halves[0][2]])
    halves.append(forward(some_walkers(orbitals, share, share, [made])))
    own, beside, facing, far, out_facing, out_far = zip(*halves)
    pieces = exchange(made)
    (sent,) = send([pieces], inward)
    next_to = [moved(pieces, [beside[i]], plane, i) for i in range(parts)]
    pieces = exchange(*made_for((2,), [far[first], out_facing[first]]))
    made = made_for((3, 0), [facing[second], beside[second], out_far[first]])
    cross = [moved(pieces, [out_facing[i], far[i]], plane, i, made[1:]) for i in range(parts)]
    landed = [moved(sent, [own[i]], plane ^ 1, i, cross) for i in range(parts)]
    pieces = exchange(made[0])
    mirror = [moved(pieces, [out_far[i], facing[i]], plane, i, cross) for i in range(parts)]
    mirror = send(mirror, along([(0, 3), (3, 0), (1, 2), (2, 1)]))
    cross = send(cross, along([(0, 2), (2, 0), (1, 3), (3, 1)]))
    next_to = send(next_to, outward)
    pieces = exchange(made[1])
    home = [moved(pieces, [own[first]], plane, first, cross)]
    home.append(moved(pieces, [own[second]], plane, second, mirror))
    return (join_rows(scalars(plane), list(zip(home, next_to, landed, cross, mirror))), log_factor)


def solution(mesh):
    placed = (
        P(None, "chol", None),
        P(None, "chol", None),
        P("grp", "chol", None),
        P("grp", None),
        P(("grp", "chol"), None, None),
    )
    return jax.shard_map(
        functools.partial(on_device, mesh.shape["chol"]),
        mesh=mesh,
        in_specs=placed,
        out_specs=(P(("grp", "chol"), None, None), P(("grp", "chol"))),
        check_vma=False,
    )
```

```python
import functools

import jax
import jax.numpy as jnp
from jax import lax
from jax.experimental import pallas as pl
from jax.experimental.pallas import tpu as pltpu
from jax.sharding import PartitionSpec as P

PLANES = 4
TILE = 16
VMEM = 60 * 1024 * 1024


def shift_terms(vbias, gauss_rows):
    xbar = jnp.clip(-0.3 * vbias, -1.0, 1.0)
    log_terms = jnp.sum(gauss_rows * xbar - 0.5 * xbar * xbar, axis=1)
    fields = (gauss_rows - xbar).astype(jnp.bfloat16)
    return (fields, log_terms)


def butterfly_sum(value, size):
    step = 1
    while step < size:
        if 2 * step < size:
            one, two, three = (
                lax.ppermute(value, "chol", [(i, i ^ (k * step)) for i in range(size)]) for k in (1, 2, 3)
            )
            value = (value + one) + (two + three)
            step *= 4
        else:
            value = value + lax.ppermute(value, "chol", [(i, i ^ step) for i in range(size)])
            step *= 2
    return value


def potential_kernel(slots, fields_ref, chol_ref, *rest):
    outs, spread = rest[-1 - slots : -1], rest[-1]
    vectors, tile, width = chol_ref.shape
    walkers = fields_ref.shape[0]

    @pl.when(pl.program_id(0) == 0)
    def _():
        shape = (vectors, vectors * tile)
        pick = lax.broadcasted_iota(jnp.int32, shape, 1) // tile == lax.broadcasted_iota(jnp.int32, shape, 0)
        wide = jnp.dot(fields_ref[...], pick.astype(jnp.bfloat16), preferred_element_type=jnp.float32)
        shape = (tile, vectors * tile)
        mine = lax.broadcasted_iota(jnp.int32, shape, 1) % tile == lax.broadcasted_iota(jnp.int32, shape, 0)
        for w in range(walkers):
            rows = jnp.where(mine, jnp.broadcast_to(wide[w : w + 1], shape), 0.0)
            spread[w * tile : (w + 1) * tile, :] = rows.astype(jnp.bfloat16)

    total = jnp.dot(
        spread[...], chol_ref[...].reshape(vectors * tile, width), preferred_element_type=jnp.float32
    )
    value = (total * 0.3).astype(jnp.bfloat16).reshape(slots, walkers // slots, tile, width)
    for i in range(slots):
        outs[i][...] = value[i]


def potential_rows(fields, chol_full, after):
    vectors, rows, width = chol_full.shape
    slots, share = len(fields), fields[0].shape[0]
    walkers = slots * share
    return pl.pallas_call(
        functools.partial(potential_kernel, slots),
        grid=(rows // TILE,),
        in_specs=[
            pl.BlockSpec((walkers, vectors), lambda b: (0, 0)),
            pl.BlockSpec((vectors, TILE, width), lambda b: (0, b, 0)),
        ]
        + [pl.BlockSpec(memory_space=pl.ANY)] * len(after),
        out_specs=[pl.BlockSpec((share, TILE, width), lambda b: (0, b, 0))] * slots,
        out_shape=[jax.ShapeDtypeStruct((share, rows, width), jnp.bfloat16)] * slots,
        scratch_shapes=[pltpu.VMEM((walkers * TILE, vectors * TILE), jnp.bfloat16)],
        compiler_params=pltpu.CompilerParams(vmem_limit_bytes=VMEM),
        cost_estimate=pl.CostEstimate(flops=60_000_000_000, bytes_accessed=1, transcendentals=0),
    )(jnp.concatenate(fields, axis=0), chol_full, *after)


def copy_kernel(source, *rest):
    rest[-1][...] = source[...]


def some_walkers(orbitals, first, walkers, after):
    _, width, occupied = orbitals.shape
    return pl.pallas_call(
        copy_kernel,
        grid=(walkers,),
        in_specs=[pl.BlockSpec((1, width, occupied), lambda w: (w + first, 0, 0))]
        + [pl.BlockSpec(memory_space=pl.ANY)] * len(after),
        out_specs=pl.BlockSpec((1, width, occupied), lambda w: (w, 0, 0)),
        out_shape=jax.ShapeDtypeStruct((walkers, width, occupied), orbitals.dtype),
        compiler_params=pltpu.CompilerParams(vmem_limit_bytes=VMEM),
        cost_estimate=pl.CostEstimate(flops=1, bytes_accessed=1, transcendentals=0),
    )(orbitals, *after)


def moved_kernel(choices, scalars, pieces, *refs):
    orbs, out = refs[:choices], refs[-1]
    rows = out.shape[1]

    def orbital_rows(index):
        if choices == 1:
            return orbs[0][index]
        return jnp.where(scalars[0] == 0, orbs[0][index], orbs[1][index])

    left = pieces[...].reshape(rows, pieces.shape[3])
    moved = jnp.dot(left, orbital_rows(0), preferred_element_type=jnp.float32)
    old = orbital_rows((0, pl.ds(pl.multiple_of(scalars[1] * rows, rows), rows)))
    out[0] = (old.astype(jnp.float32) + moved).astype(jnp.bfloat16)


def moved_rows(pieces, orbs, scalars, first, after=()):
    choices = len(orbs)
    lanes, _, rows, width = pieces.shape
    walkers, _, occupied = orbs[0].shape
    return pl.pallas_call(
        functools.partial(moved_kernel, choices),
        grid_spec=pltpu.PrefetchScalarGridSpec(
            num_scalar_prefetch=1,
            grid=(walkers,),
            in_specs=[pl.BlockSpec((lanes, 1, rows, width), lambda w, s: (0, w + first, 0, 0))]
            + [pl.BlockSpec((1, width, occupied), lambda w, s: (w, 0, 0))] * choices
            + [pl.BlockSpec(memory_space=pl.ANY)] * len(after),
            out_specs=pl.BlockSpec((1, lanes * rows, occupied), lambda w, s: (w, 0, 0)),
        ),
        out_shape=jax.ShapeDtypeStruct((walkers, lanes * rows, occupied), jnp.bfloat16),
        compiler_params=pltpu.CompilerParams(vmem_limit_bytes=VMEM),
        cost_estimate=pl.CostEstimate(flops=15_000_000_000, bytes_accessed=1, transcendentals=0),
    )(scalars, pieces, *orbs, *after)


def join_kernel(parts, scalars, *refs):
    out = refs[-1]
    rows = refs[0].shape[1]
    share = refs[0].shape[0]

    for part in range(parts):
        own, beside, sent, cross, mirror = refs[part * 5 : part * 5 + 5]
        walkers = pl.ds(part * share, share)

        def put(value, k):
            out[walkers, pl.ds(pl.multiple_of((scalars[1] ^ k) * rows, rows), rows), :] = value

        put(own[...], 0)
        put(jnp.where(scalars[0] == 0, beside[...], sent[...]), 1)
        put(cross[...], 2)
        put(mirror[...], 3)


def join_rows(scalars, parts):
    walkers, rows, occupied = parts[0][0].shape
    columns = 128 if occupied % 128 == 0 else occupied
    return pl.pallas_call(
        functools.partial(join_kernel, len(parts)),
        grid_spec=pltpu.PrefetchScalarGridSpec(
            num_scalar_prefetch=1,
            grid=(occupied // columns,),
            in_specs=[pl.BlockSpec((walkers, rows, columns), lambda c, s: (0, 0, c))] * (5 * len(parts)),
            out_specs=pl.BlockSpec((len(parts) * walkers, PLANES * rows, columns), lambda c, s: (0, 0, c)),
        ),
        out_shape=jax.ShapeDtypeStruct((len(parts) * walkers, PLANES * rows, occupied), jnp.bfloat16),
        compiler_params=pltpu.CompilerParams(vmem_limit_bytes=VMEM),
    )(scalars, *(block for part in parts for block in part))


def on_device(size, chol_full, chol_half, green, gauss, orbitals):
    walkers = green.shape[0]
    owned = orbitals.shape[0]
    vectors = chol_half.shape[0]
    lanes = size // PLANES
    me = lax.axis_index("chol")
    plane, lane = me // lanes, me % lanes
    inner = ((plane == 1) | (plane == 2)).astype(jnp.int32)

    def along(targets):
        return [(a * lanes + k, b * lanes + k) for a, b in targets for k in range(lanes)]

    inward = along([(0, 1), (3, 2)])
    outward = along([(1, 0), (2, 3)])
    middle = along([(1, 2), (2, 1)])

    def send(arrays, targets):
        return [lax.ppermute(a, "chol", targets) for a in arrays]

    parts = 2
    share = owned // parts

    def forward(mine):
        beside, facing = send([mine], inward), send([mine], middle)
        far, out_facing = send(beside, middle), send(facing, outward)
        return mine, beside[0], facing[0], far[0], out_facing[0], send(far, outward)[0]

    halves = [forward(some_walkers(orbitals, 0, share, []))]

    partial_value = lax.dot_general(
        green.reshape(walkers, -1),
        chol_half.reshape(vectors, -1),
        (((1,), (1,)), ((), ())),
        preferred_element_type=jnp.float32,
    )
    vbias = butterfly_sum(partial_value, size)
    fields, log_terms = shift_terms(vbias, gauss)
    log_factor = lax.dynamic_slice_in_dim(log_terms, me * owned, owned, 0)
    fields = fields.reshape(PLANES, lanes * owned, vectors)
    rows, width = chol_full.shape[1:]
    groups = [[p * lanes + k for k in range(lanes)] for p in range(PLANES)]

    def made_for(slots, after):
        chosen = [lax.dynamic_index_in_dim(fields, plane ^ slot, 0, keepdims=False) for slot in slots]
        return potential_rows(chosen, chol_full, after)

    def exchange(made):
        return lax.all_to_all(made, "chol", 0, 0, axis_index_groups=groups, tiled=True).reshape(lanes, owned, rows, width)

    def scalars(rows_of):
        return jnp.stack([inner, rows_of]).astype(jnp.int32)

    def moved(pieces, choices, rows_of, i, after=()):
        return moved_rows(pieces, choices, scalars(rows_of), i * share, after)

    first, second = range(parts)
    (made,) = made_for((1,), [halves[0][1], halves[0][2]])
    halves.append(forward(some_walkers(orbitals, share, share, [made])))
    own, beside, facing, far, out_facing, out_far = zip(*halves)
    pieces = exchange(made)
    (sent,) = send([pieces], inward)
    next_to = [moved(pieces, [beside[i]], plane, i) for i in range(parts)]
    pieces = exchange(*made_for((2,), [far[first], out_facing[first]]))
    made = made_for((3, 0), [facing[second], beside[second], out_far[first]])
    cross = [moved(pieces, [out_facing[i], far[i]], plane, i, made[1:]) for i in range(parts)]
    landed = [moved(sent, [own[i]], plane ^ 1, i, cross) for i in range(parts)]
    pieces = exchange(made[0])
    mirror = [moved(pieces, [out_far[i], facing[i]], plane, i, cross) for i in range(parts)]
    mirror = send(mirror, along([(0, 3), (3, 0), (1, 2), (2, 1)]))
    cross = send(cross, along([(0, 2), (2, 0), (1, 3), (3, 1)]))
    next_to = send(next_to, outward)
    pieces = exchange(made[1])
    home = [moved(pieces, [own[i]], plane, i, [*cross, mirror[first]]) for i in range(parts)]
    return (join_rows(scalars(plane), list(zip(home, next_to, landed, cross, mirror))), log_factor)


def solution(mesh):
    placed = (
        P(None, "chol", None),
        P(None, "chol", None),
        P("grp", "chol", None),
        P("grp", None),
        P(("grp", "chol"), None, None),
    )
    return jax.shard_map(
        functools.partial(on_device, mesh.shape["chol"]),
        mesh=mesh,
        in_specs=placed,
        out_specs=(P(("grp", "chol"), None, None), P(("grp", "chol"))),
        check_vma=False,
    )
```
